32 devices in a mesh: row: 16 (over z, y, core), col: 2 (over x).
Axes of the slice: x: 2, y: 2, z: 4, core: 2. Of those that a mesh axis runs over, the one named last changes fastest.
Arguments:
- obs_summaries: bfloat16 [8192, 256], P(('row', 'col')), may hold values from -6 to 6
- sim_summaries: bfloat16 [4096, 256], P('row'), may hold values from -6 to 6
- neighbours: int32 [8192, 16], P(('row', 'col')), may hold values from 0 to 4095
- field: bfloat16 [4096, 2048], P('row', 'col'), may hold values from -6 to 6
Outputs:
- posterior: bfloat16 [8192, 2048], P('row', 'col')
The draws below stay inside these ranges and needn't reach their ends.
Inputs may be any that keep to these rules, and one draw needn't show every extreme that they name: `neighbours`: each entry names a row of sim_summaries.
All inputs are finite; a program needn't handle non-finite values.
Results may differ from the reference program's by a relative error of at most 0.005.
Values may be sent and summed in bfloat16 or wider, within the bound.
No kernel may reach another device: no remote copies, remote signals or barrier semaphores. Data moves between devices by JAX's collectives and lax.ppermute only.
A program may use at most 128 MiB of HBM per device.

```python
import jax
import jax.numpy as jnp
from jax import lax

DS = 256
KNN = 16
OBS_DEV = 512
SIM_DEV = 256
NOBS = 8192
NSIM = 4096
NCELL = 2048
N_ROW = 16


def touch_ends(drawn, stream_key, smallest, largest):
    longest = drawn.shape.index(max(drawn.shape))
    spots = []
    for shift in (0, 1):
        where = [jax.random.randint(jax.random.fold_in(stream_key, axis), (), 0, length) for axis, length in enumerate(drawn.shape)]
        where[longest] = (where[longest] + shift) % drawn.shape[longest]
        spots.append(tuple(where))
    return drawn.at[spots[0]].set(smallest).at[spots[1]].set(largest)


def block_levels(stream_key, dims, cuts, least, largest):
    def one(dim, blocks):
        draws = jax.random.uniform(jax.random.fold_in(jax.random.fold_in(stream_key, 6), dim), (blocks,), jnp.float32, least / len(cuts), largest / len(cuts))
        return jnp.repeat(jnp.exp(draws), dims[dim] // blocks).reshape((-1,) + (1,) * (len(dims) - dim - 1))

    loudness = one(*cuts[0])
    for cut in cuts[1:]:
        loudness = loudness * one(*cut)
    return loudness


def scatter_about(rng, extent, spread, reach, shards=(), kind=jnp.bfloat16):
    entries = spread * jax.random.normal(rng, extent, jnp.float32)
    if shards:
        entries = entries * block_levels(rng, extent, shards, -0.22, 0.18)
    return jnp.clip(entries, -reach, reach).astype(kind)


def setup_inputs(seed: int = 0) -> dict:
    keys = jax.random.split(jax.random.key(seed), 5)
    return {
        "obs_summaries": scatter_about(keys[0], (NOBS, DS), 1.0, 6.0, ((0, 32),)),
        "sim_summaries": scatter_about(keys[1], (NSIM, DS), 1.0, 6.0, ((0, 16),)),
        "neighbours": touch_ends(jax.random.randint(keys[2], (NOBS, KNN), 0, NSIM), jax.random.fold_in(keys[2], 1), 0, NSIM - 1).astype(jnp.int32),
        "field": scatter_about(keys[3], (NSIM, NCELL), 1.0, 6.0, ((0, 16), (1, 2))),
    }


SHARPNESS = 32.0
EPSILON = 1e-6


def neighbour_widths(obs_rows, index_rows, sims_full, sim_square):
    obs_float = obs_rows.astype(jnp.float32)
    near_rows = sims_full[index_rows].astype(jnp.float32)
    inner_prod = jnp.einsum("rd,rkd->rk", obs_float, near_rows)
    obs_square = jnp.sum(obs_float * obs_float, axis=1)
    distance = obs_square[:, None] + sim_square[index_rows] - 2.0 * inner_prod
    return jnp.mean(distance, axis=1) + EPSILON


def reference(obs_summaries, sim_summaries, neighbours, field):
    sim_float = sim_summaries.astype(jnp.float32)
    sim_square = jnp.sum(sim_float * sim_float, axis=1)
    obs_blocks = obs_summaries.reshape(N_ROW, OBS_DEV, DS)
    index_blocks = neighbours.reshape(N_ROW, OBS_DEV, KNN)
    sim_blocks = sim_summaries.reshape(N_ROW, SIM_DEV, DS)
    square_blocks = sim_square.reshape(N_ROW, SIM_DEV)
    field_blocks = field.reshape(N_ROW, SIM_DEV, NCELL)

    def one_block(inputs):
        obs_rows, index_rows = inputs
        width = neighbour_widths(obs_rows, index_rows, sim_summaries, sim_square)
        obs_float = obs_rows.astype(jnp.float32)
        obs_square = jnp.sum(obs_float * obs_float, axis=1)

        def step_sims(carry, pieces):
            numer, total = carry
            sim_piece, square_piece, field_piece = pieces
            distance = obs_square[:, None] + square_piece[None, :] - 2.0 * jnp.dot(obs_rows, sim_piece.T, preferred_element_type=jnp.float32)
            weight = jnp.exp(-SHARPNESS * distance / width[:, None])
            numer = numer + jnp.dot(weight.astype(jnp.bfloat16), field_piece, preferred_element_type=jnp.float32)
            total = total + jnp.sum(weight, axis=1)
            return (numer, total), None

        start = (jnp.zeros((OBS_DEV, NCELL), jnp.float32), jnp.zeros((OBS_DEV,), jnp.float32))
        (numer, total), _ = lax.scan(step_sims, start, (sim_blocks, square_blocks, field_blocks))
        return (numer / total[:, None]).astype(jnp.bfloat16)

    result = lax.map(one_block, (obs_blocks, index_blocks))
    return result.reshape(NOBS, NCELL)
```

```python
import functools
import math

import jax
import jax.numpy as jnp
from jax import lax
from jax.experimental import pallas as pl
from jax.experimental.pallas import tpu as pltpu
from jax.sharding import PartitionSpec as P

SHARPNESS = 32.0
EPSILON = 1e-06
LANES = 128
CORE_BIT = 1
Y_BIT = 2
VMEM = pl.BlockSpec(memory_space=pltpu.VMEM)
SMEM = pl.BlockSpec(memory_space=pltpu.SMEM)


def swap(value, axis, size, bit):
    return lax.ppermute(value, axis, [(i, i ^ bit) for i in range(size)])


def gather_steps(size):
    n_z = size // 4
    steps = []
    if n_z == 4:
        across = [(i ^ 12) if (i >> 2) in (1, 2) else (i ^ Y_BIT) for i in range(size)]
        inside = [i ^ 4 for i in range(size)]
        for sent, first in ((0, inside), (0, across), (1, across), (2, inside), (3, inside), (4, across), (5, across)):
            second = across if first is inside else inside
            steps.append((sent, [(i, second[i] if i & CORE_BIT else first[i]) for i in range(size)]))
        return steps
    held = 1
    for bit in [Y_BIT << k for k in range(n_z.bit_length())]:
        steps += [(sent, [(i, i ^ bit) for i in range(size)]) for sent in range(held)]
        held *= 2
    return steps


def owners(size):
    held = [[i] for i in range(size)]
    for sent, pairs in gather_steps(size):
        source = {target: i for i, target in pairs}
        moved = [held[source[i]][sent] for i in range(size)]
        for i in range(size):
            held[i].append(moved[i])
    held = [held[i] + held[i ^ CORE_BIT] for i in range(size)]
    assert all(sorted(row) == list(range(size)) for row in held)
    return held


def gather_rows(value, size, after=None):
    blocks = [value]
    for k, (sent, pairs) in enumerate(gather_steps(size)):
        block = blocks[sent]
        if after and k in after:
            block = lax.optimization_barrier((block, after[k]))[0]
        blocks.append(lax.ppermute(block, "row", pairs))
    return blocks, [swap(block, "row", size, CORE_BIT) for block in blocks]


def weight_kernel(n_sim, n_piece, owner_ref, *refs):
    obs_in, near_in = refs[:n_piece], refs[n_piece : 2 * n_piece]
    sims = refs[2 * n_piece : 2 * n_piece + n_sim]
    weight_out, total_out, obs_scr, low_scr, high_scr, value_scr = refs[2 * n_piece + n_sim :]
    my_row, my_col = lax.axis_index("row"), lax.axis_index("col")
    rows = obs_in[0].shape[0]
    near = near_in[0].shape[0]
    depth = sims[0].shape[0]
    n_obs = n_piece * rows
    for i in range(n_piece):
        slot = lax.bitwise_xor(my_col, i)
        at = pl.ds(pl.multiple_of(slot * rows, rows), rows)
        obs_scr[at, :] = obs_in[i][...]
        index = near_in[i][...].astype(jnp.float32).T.astype(jnp.int32)
        pad = jnp.zeros((rows, LANES - near), jnp.int32)
        high_scr[at, :] = jnp.concatenate([index // LANES, pad - 1], axis=1)
        low_scr[at, :] = jnp.concatenate([index % LANES, pad], axis=1)
    obs = obs_scr[...]
    obs_float = obs.astype(jnp.float32)
    obs_square = jnp.sum(obs_float * obs_float, axis=1, keepdims=True)
    low, high = low_scr[...], high_scr[...]
    near_sum = jnp.zeros((n_obs, LANES), jnp.float32)
    for b in range(n_sim):
        block = sims[b][...]
        squares = block.astype(jnp.float32)
        squares = squares * squares
        folded = squares[:, :LANES]
        for g in range(1, block.shape[1] // LANES):
            folded += squares[:, g * LANES : (g + 1) * LANES]
        sim_square = jnp.sum(folded.T, axis=0, keepdims=True)
        cross = lax.dot_general(obs, block, (((1,), (1,)), ((), ())), preferred_element_type=jnp.float32)
        values = sim_square - 2.0 * cross
        value_scr[:, b * depth : (b + 1) * depth] = values
        owner = owner_ref[my_row * n_sim + b] * (depth // LANES)
        for g in range(depth // LANES):
            found = jnp.take_along_axis(values[:, g * LANES : (g + 1) * LANES], low, axis=1)
            near_sum += jnp.where(high == owner + g, found, 0.0)
    width = obs_square + jnp.sum(near_sum, axis=1, keepdims=True) / near + EPSILON
    factor = (-SHARPNESS * math.log2(math.e)) / width
    total = jnp.zeros((n_obs, LANES), jnp.float32)
    for b in range(n_sim):
        at = slice(b * depth, (b + 1) * depth)
        weight = jnp.exp2(factor * (obs_square + value_scr[:, at]))
        weight_out[:, at] = weight.astype(jnp.bfloat16)
        for g in range(depth // LANES):
            total += weight[:, g * LANES : (g + 1) * LANES]
    total_out[...] = jnp.broadcast_to(jnp.sum(total, axis=1, keepdims=True), total.shape)


def product_kernel(columns, depth, first, last, weight, *refs):
    blocks, rest, out = refs[: len(columns)], refs[len(columns) : -1], refs[-1]
    so_far = None if first else rest[-1]
    total_ref = rest[0] if last else None
    cells = out.shape[1]
    step = min(cells, 256)
    for j in range(cells // step):
        at = slice(j * step, (j + 1) * step)
        total = None if so_far is None else so_far[:, at]
        for column, block in zip(columns, blocks):
            term = jnp.dot(
                weight[:, column * depth : (column + 1) * depth], block[:, at], preferred_element_type=jnp.float32
            )
            total = term if total is None else total + term
        if total_ref is not None:
            total = total / total_ref[:, :1]
        out[:, at] = total.astype(out.dtype)


def call(kernel, vmem, **kw):
    return pl.pallas_call(kernel, compiler_params=pltpu.CompilerParams(vmem_limit_bytes=vmem << 20), **kw)


def per_device(n_row, n_col, obs_summaries, sim_summaries, neighbours, field):
    f32, bf16 = jnp.float32, jnp.bfloat16
    rows, dims = obs_summaries.shape
    depth, cells = field.shape

    obs, near = [obs_summaries], [neighbours.T]
    for k in range(n_col.bit_length() - 1):
        obs = obs + [swap(p, "col", n_col, 1 << k) for p in obs]
        near = near + [swap(p, "col", n_col, 1 << k) for p in near]

    own_sims, other_sims = gather_rows(sim_summaries, n_row)
    sims = own_sims + other_sims
    n_sim, n_piece = len(sims), len(obs)
    owner_table = jnp.array(owners(n_row), jnp.int32).reshape(-1)
    n_obs = n_piece * rows
    weight, total = call(
        functools.partial(weight_kernel, n_sim, n_piece),
        40,
        in_specs=[SMEM] + [VMEM] * (2 * n_piece + n_sim),
        out_specs=[VMEM] * 2,
        out_shape=[
            jax.ShapeDtypeStruct((n_obs, n_sim * depth), bf16),
            jax.ShapeDtypeStruct((n_obs, LANES), f32),
        ],
        scratch_shapes=[
            pltpu.VMEM((n_obs, dims), bf16),
            pltpu.VMEM((n_obs, LANES), jnp.int32),
            pltpu.VMEM((n_obs, LANES), jnp.int32),
            pltpu.VMEM((n_obs, n_sim * depth), f32),
        ],
        cost_estimate=pl.CostEstimate(
            flops=4 * n_obs * n_sim * depth * dims,
            bytes_accessed=8 << 20,
            transcendentals=n_obs * n_sim * depth,
        ),
        name="weights",
    )(owner_table, *obs, *near, *sims)

    after = {k: own_sims[2 * k + 1] for k in range(len(own_sims) // 2)}
    own_blocks, other_blocks = gather_rows(field, n_row, after)
    n_half = n_sim // 2
    cuts = (0, n_half // 2, n_half - 1, n_half)
    groups = [tuple(range(a, b)) for a, b in zip(cuts[:-1], cuts[1:])]
    result = None
    for g, group in enumerate(groups):
        columns = group + tuple(k + n_half for k in group)
        blocks = [own_blocks[k] for k in group] + [other_blocks[k] for k in group]
        last = g == len(groups) - 1
        extra = ([total] if last else []) + ([] if result is None else [result])
        result = call(
            functools.partial(product_kernel, columns, depth, g == 0, last),
            28,
            in_specs=[VMEM] * (1 + len(columns) + len(extra)),
            out_specs=VMEM,
            out_shape=jax.ShapeDtypeStruct((n_obs, cells), bf16 if last else f32),
            cost_estimate=pl.CostEstimate(
                flops=2 * n_obs * len(columns) * depth * cells,
                bytes_accessed=len(columns) * depth * (n_obs + cells) * 2,
                transcendentals=0,
            ),
            name="product",
        )(weight, *blocks, *extra)
    return result


def solution(mesh):
    return jax.shard_map(
        functools.partial(per_device, mesh.shape["row"], mesh.shape["col"]),
        mesh=mesh,
        in_specs=(
            P(("row", "col"), None),
            P("row", None),
            P(("row", "col"), None),
            P("row", "col"),
        ),
        out_specs=P("row", "col"),
        check_vma=False,
    )
```

```python
import functools
import math

import jax
import jax.numpy as jnp
from jax import lax
from jax.experimental import pallas as pl
from jax.experimental.pallas import tpu as pltpu
from jax.sharding import PartitionSpec as P

SHARPNESS = 32.0
EPSILON = 1e-06
LANES = 128
CORE_BIT = 1
Y_BIT = 2
VMEM = pl.BlockSpec(memory_space=pltpu.VMEM)
SMALL = pl.CostEstimate(flops=1024, bytes_accessed=1024, transcendentals=0)


def swap(value, axis, size, bit):
    return lax.ppermute(value, axis, [(i, i ^ bit) for i in range(size)])


def gather_steps(size):
    n_z = size // 4
    steps = []
    if n_z == 4:
        across = [(i ^ 12) if (i >> 2) in (1, 2) else (i ^ Y_BIT) for i in range(size)]
        inside = [i ^ 4 for i in range(size)]
        for sent, first in ((0, inside), (0, across), (1, across), (2, inside), (3, inside), (4, across), (5, across)):
            second = across if first is inside else inside
            steps.append((sent, [(i, second[i] if i & CORE_BIT else first[i]) for i in range(size)]))
        return steps
    held = 1
    for bit in [Y_BIT << k for k in range(n_z.bit_length())]:
        steps += [(sent, [(i, i ^ bit) for i in range(size)]) for sent in range(held)]
        held *= 2
    return steps


def owners(size):
    held = [[i] for i in range(size)]
    for sent, pairs in gather_steps(size):
        source = {target: i for i, target in pairs}
        moved = [held[source[i]][sent] for i in range(size)]
        for i in range(size):
            held[i].append(moved[i])
    held = [held[i] + held[i ^ CORE_BIT] for i in range(size)]
    assert all(sorted(row) == list(range(size)) for row in held)
    return held


PAIR_STEPS = ((False, 4, 8), (False, 14, 2), (True, 2, 4), (True, 2, 2))
PAIR_OFFSETS = ((4, 14, 6), (8, 2, 12, 10))

ORDER = {
    "F1": ("S1", "S2"),
    "F2": ("S1", "S2", "S3", "S4"),
    "F3": ("S3", "S4"),
    "F4": ("S3", "S4"),
    "F5": ("Sx",),
    "F7": ("K",),
    "D7": ("P2",),
    "Sx": ("Ox",),
    "ScSx": ("Sx",),
}
MERGED = False
GROUPS = (4, 3, 1)


class Work:
    def __init__(self, order):
        self.order, self.made, self.makers = order, {}, {}

    def add(self, name, operand, make):
        self.makers[name] = (operand, make)

    def get(self, name):
        if name not in self.made:
            operand, make = self.makers[name]
            value = operand()
            others = [self.get(other) for other in self.order.get(name, ())]
            if others:
                value = lax.optimization_barrier((value, others))[0]
            self.made[name] = make(value)
        return self.made[name]


def share_sims(work, sims, obs, codes, n_row, n_col):
    rows, depth = obs.shape[0], sims.shape[0]

    def add_swap(name, of, axis, size, bit):
        work.add(name, lambda: work.get(of), lambda value: swap(value, axis, size, bit))

    work.add("own", lambda: sims, lambda value: value)
    work.add("obs0", lambda: obs, lambda value: value)
    work.add("codes0", lambda: codes, lambda value: value)
    if (n_row, n_col) != (16, 2):
        names = ["own"]
        for k, (sent, pairs) in enumerate(gather_steps(n_row)):
            names.append(f"S{k + 1}")
            work.add(
                names[-1],
                lambda of=names[sent]: work.get(of),
                lambda value, pairs=pairs: lax.ppermute(value, "row", pairs),
            )
        names += [f"{name}c" for name in names]
        for name in names[n_row // 2 :]:
            add_swap(name, name[:-1], "row", n_row, CORE_BIT)
        for what in ("obs", "codes"):
            names.append(f"{what}0")
            for k in range(1, n_col):
                top = 1 << (k.bit_length() - 1)
                names.append(f"{what}{k}")
                add_swap(names[-1], f"{what}{k ^ top}", "col", n_col, top)
        at = [(k, 0) for k in range(len(names))]
        n = n_row + n_col
        table = [held for held in owners(n_row) for _ in range(n_col)]
        return names, [(a, a) for a in at[:n_row]], at[n_row:n], at[n:], table
    for k, (again, off_a, off_b) in enumerate(PAIR_STEPS):
        pairs = [(2 * r + c, 2 * (r ^ (off_b if c else off_a)) + c) for r in range(n_row) for c in range(2)]
        work.add(
            f"S{k + 1}",
            lambda of="S1" if again else "own": work.get(of),
            lambda value, pairs=pairs: lax.ppermute(value, ("row", "col"), pairs),
        )
    arrived = lambda: [work.get(f"S{k + 1}") for k in range(4)]
    if MERGED:
        work.add("mine", lambda: arrived() + [obs, codes], lambda parts: jnp.concatenate(parts, axis=0))
        obs_at = [(1, 4 * depth), (2, 4 * depth)]
        names = ["own", "mine", "Sx"]
    else:
        work.add("mine", arrived, lambda parts: jnp.concatenate(parts, axis=0))
        work.add("both", lambda: [obs, codes], lambda parts: jnp.concatenate(parts, axis=0))
        add_swap("Ox", "both", "col", n_col, 1)
        names = ["own", "mine", "Sx"]
        obs_at = [(6, 0), (7, 0)]
    add_swap("Sx", "mine", "col", n_col, 1)
    blocks = [((0, 0), (0, 0))]
    for k in range(3):
        blocks += [((1, k * depth),) * 2, ((2, k * depth),) * 2]
    blocks += [((2, 3 * depth), (1, 3 * depth))]
    blocks += [tuple((s + len(names), k) for s, k in block) for block in blocks]
    table = []
    for r in range(n_row):
        for c in range(2):
            here, there = PAIR_OFFSETS[c], PAIR_OFFSETS[1 - c]
            offs = [0] + [o for k in range(3) for o in (here[k], there[k])] + [PAIR_OFFSETS[1][3]]
            table.append([r ^ o for o in offs] + [r ^ CORE_BIT ^ o for o in offs])
            assert sorted(table[-1]) == list(range(n_row))
    for name in tuple(names):
        names.append(f"Sc{name}")
        add_swap(names[-1], name, "row", n_row, CORE_BIT)
    if not MERGED:
        names += ["both", "Ox"]
    return names, blocks, obs_at, [(s, k + rows) for s, k in obs_at], table


def kinds_of_place(n_row, n_col, table):
    held = owners(n_row)
    kind_of, seen = [], []
    for r in range(n_row):
        offsets = [r ^ owner for owner in held[r]]
        kind_of.append([])
        for c in range(n_col):
            what = (offsets, [held[r].index(owner) for owner in table[r * n_col + c]])
            if what not in seen:
                seen.append(what)
            kind_of[-1].append(seen.index(what))
    return kind_of, [w[0] for w in seen], [w[1] for w in seen]


def choose(index, options):
    if all(o == options[0] for o in options):
        return options[0]
    out = jnp.int32(options[0])
    for i, option in enumerate(options[1:], 1):
        out = jnp.where(index == i, option, out)
    return out


def weight_kernel(blocks, obs_at, codes_at, kinds, depth, rows, near, n_in, *refs):
    n_sim, n_piece = len(blocks), len(obs_at)
    arrays, (weight_out, total_out) = refs[:n_in], refs[n_in : n_in + 2]
    obs_scr, low_scr, high_scr, value_scr, square_scr, factor_scr, owner_scr = refs[n_in + 2 :]
    my_row, my_col = lax.axis_index("row"), lax.axis_index("col")
    n_obs = n_piece * rows
    groups = depth // LANES

    kind_of, offsets, places = kinds
    n_col = len(kind_of[0])
    kind = choose(my_row * n_col + my_col, [k for row in kind_of for k in row])
    for b in range(n_sim):
        owner_scr[b] = lax.bitwise_xor(my_row, choose(kind, [o[b] for o in offsets])) * groups

    for i in range(n_piece):
        at = pl.ds(pl.multiple_of(lax.bitwise_xor(my_col, i) * rows, rows), rows)
        (s, k), (t, m) = obs_at[i], codes_at[i]
        obs_scr[at, :] = arrays[s][k : k + rows, :]
        codes = arrays[t][m : m + 2 * near, :rows].astype(jnp.float32).T.astype(jnp.int32)
        pad = jnp.zeros((rows, LANES - near), jnp.int32)
        high_scr[at, :] = jnp.concatenate([codes[:, :near], pad - 1], axis=1)
        low_scr[at, :] = jnp.concatenate([codes[:, near:], pad], axis=1)
    obs = obs_scr[...]
    obs_float = obs.astype(jnp.float32)
    square_scr[...] = jnp.broadcast_to(jnp.sum(obs_float * obs_float, axis=1, keepdims=True), (n_obs, LANES))

    for b, at_cols in enumerate(blocks):
        block, at_one = [arrays[s][k : k + depth, :] for s, k in at_cols]
        if at_cols[0] != at_cols[1]:
            block = jnp.where(my_col == 0, block, at_one)
        squares = block.astype(jnp.float32)
        squares = squares * squares
        folded = squares[:, :LANES]
        for g in range(1, block.shape[1] // LANES):
            folded += squares[:, g * LANES : (g + 1) * LANES]
        sim_square = jnp.sum(folded.T, axis=0, keepdims=True)
        cross = lax.dot_general(obs, block, (((1,), (1,)), ((), ())), preferred_element_type=jnp.float32)
        place = choose(kind, [p[b] for p in places]) * groups
        for g in range(groups):
            at = slice(g * LANES, (g + 1) * LANES)
            value_scr[place + g] = sim_square[:, at] - 2.0 * cross[:, at]

    tile = 8
    some = min(n_obs, 64)

    def add_near(t, carry):
        for r in range(some // tile):
            at = pl.ds(pl.multiple_of(t * some + r * tile, tile), tile)
            low, high = low_scr[at, :], high_scr[at, :]
            total = jnp.zeros((tile, LANES), jnp.float32)
            for c in range(n_sim * groups):
                found = jnp.take_along_axis(value_scr[c, at, :], low, axis=1)
                total += jnp.where(high == owner_scr[c // groups] + c % groups, found, 0.0)
            factor_scr[at, :] = total
        return carry

    lax.fori_loop(0, n_obs // some, add_near, 0)
    width = square_scr[...] + jnp.sum(factor_scr[...], axis=1, keepdims=True) / near + EPSILON
    factor_scr[...] = (-SHARPNESS * math.log2(math.e)) / width
    part = min(n_obs, 32)

    def weigh(t, carry):
        at = pl.ds(pl.multiple_of(t * part, part), part)
        factor, square = factor_scr[at, :], square_scr[at, :]
        total = jnp.zeros((part, LANES), jnp.float32)
        for c in range(n_sim * groups):
            weight = jnp.exp2(factor * (square + value_scr[c, at, :]))
            weight_out[c // groups, at, c % groups * LANES : (c % groups + 1) * LANES] = weight.astype(jnp.bfloat16)
            total += weight
        total_out[at, :] = total
        return carry

    lax.fori_loop(0, n_obs // part, weigh, 0)
    total_out[...] = jnp.broadcast_to(jnp.sum(total_out[...], axis=1, keepdims=True), total_out.shape)


def product_kernel(columns, first, last, weight, *refs):
    blocks, rest, out = refs[: len(columns)], refs[len(columns) : -1], refs[-1]
    so_far = None if first else rest[-1]
    total_ref = rest[0] if last else None
    cells = out.shape[1]
    step = min(cells, 256)
    for j in range(cells // step):
        at = slice(j * step, (j + 1) * step)
        total = None if so_far is None else so_far[:, at]
        for column, block in zip(columns, blocks):
            term = jnp.dot(
                weight[column], block[:, at], preferred_element_type=jnp.float32
            )
            total = term if total is None else total + term
        if total_ref is not None:
            total = total / total_ref[:, :1]
        out[:, at] = total.astype(out.dtype)


def call(kernel, vmem, **kw):
    return pl.pallas_call(kernel, compiler_params=pltpu.CompilerParams(vmem_limit_bytes=vmem << 20), **kw)


def per_device(n_row, n_col, obs_summaries, sim_summaries, neighbours, field):
    f32, bf16 = jnp.float32, jnp.bfloat16
    rows, dims = obs_summaries.shape
    depth, cells = field.shape

    index = neighbours.T
    codes = jnp.concatenate([index // LANES, index % LANES], axis=0).astype(bf16)
    work = Work(ORDER if (n_row, n_col) == (16, 2) else {})
    names, at_blocks, at_obs, at_codes, table = share_sims(work, sim_summaries, obs_summaries, codes, n_row, n_col)
    n_sim, n_obs = n_row, n_col * rows
    kinds = kinds_of_place(n_row, n_col, table)
    weigh = call(
        functools.partial(
            weight_kernel, at_blocks, at_obs, at_codes, kinds, depth, rows, neighbours.shape[1], len(names)
        ),
        40,
        in_specs=[VMEM] * len(names),
        out_specs=[VMEM] * 2,
        out_shape=[
            jax.ShapeDtypeStruct((n_sim, n_obs, depth), bf16),
            jax.ShapeDtypeStruct((n_obs, LANES), f32),
        ],
        scratch_shapes=[
            pltpu.VMEM((n_obs, dims), bf16),
            pltpu.VMEM((n_obs, LANES), jnp.int32),
            pltpu.VMEM((n_obs, LANES), jnp.int32),
            pltpu.VMEM((n_sim * depth // LANES, n_obs, LANES), f32),
            pltpu.VMEM((n_obs, LANES), f32),
            pltpu.VMEM((n_obs, LANES), f32),
            pltpu.SMEM((n_sim,), jnp.int32),
        ],
        cost_estimate=SMALL,
        name="weights",
    )
    work.add("K", lambda: [work.get(name) for name in names], lambda arrays: weigh(*arrays))

    n_half = n_sim // 2
    work.add("F0", lambda: field, lambda value: value)
    for k, (sent, pairs) in enumerate(gather_steps(n_row)):
        work.add(
            f"F{k + 1}",
            lambda sent=sent: work.get(f"F{sent}"),
            lambda value, pairs=pairs: lax.ppermute(value, "row", pairs),
        )
    for k in range(n_half):
        work.add(f"D{k}", lambda k=k: work.get(f"F{k}"), lambda value: swap(value, "row", n_row, CORE_BIT))

    def product(first, last, parts):
        done, (weight, total), before, both = last == n_half, *parts
        columns = [*range(first, last), *range(n_half + first, n_half + last)]
        extra = ([total] if done else []) + ([] if before is None else [before])
        return call(
            functools.partial(product_kernel, columns, before is None, done),
            28,
            in_specs=[VMEM] * (1 + len(both) + len(extra)),
            out_specs=VMEM,
            out_shape=jax.ShapeDtypeStruct((n_obs, cells), bf16 if done else f32),
            cost_estimate=SMALL,
            name="product",
        )(weight, *both, *extra)

    groups = GROUPS if n_half == sum(GROUPS) else (n_half // 2, n_half - n_half // 2 - 1, 1)
    first = 0
    for g, count in enumerate(groups):
        at = range(first, first + count)
        work.add(
            f"P{g + 1}",
            lambda g=g, at=at: (
                work.get("K"),
                work.get(f"P{g}") if g else None,
                [work.get(f"F{k}") for k in at] + [work.get(f"D{k}") for k in at],
            ),
            lambda parts, at=at: product(at.start, at.stop, parts),
        )
        first += count
    return work.get(f"P{len(groups)}")


def solution(mesh):
    return jax.shard_map(
        functools.partial(per_device, mesh.shape["row"], mesh.shape["col"]),
        mesh=mesh,
        in_specs=(
            P(("row", "col"), None),
            P("row", None),
            P(("row", "col"), None),
            P("row", "col"),
        ),
        out_specs=P("row", "col"),
        check_vma=False,
    )
```

```python
import functools
import math

import jax
import jax.numpy as jnp
from jax import lax
from jax.experimental import pallas as pl
from jax.experimental.pallas import tpu as pltpu
from jax.sharding import PartitionSpec as P

SHARPNESS = 32.0
EPSILON = 1e-06
LANES = 128
CORE_BIT = 1
Y_BIT = 2
VMEM = pl.BlockSpec(memory_space=pltpu.VMEM)
SMALL = pl.CostEstimate(flops=1024, bytes_accessed=1024, transcendentals=0)


def swap(value, axis, size, bit):
    return lax.ppermute(value, axis, [(i, i ^ bit) for i in range(size)])


def gather_steps(size):
    n_z = size // 4
    steps = []
    if n_z == 4:
        across = [(i ^ 12) if (i >> 2) in (1, 2) else (i ^ Y_BIT) for i in range(size)]
        inside = [i ^ 4 for i in range(size)]
        for sent, first in ((0, inside), (0, across), (1, across), (2, inside), (3, inside), (4, across), (5, across)):
            second = across if first is inside else inside
            steps.append((sent, [(i, second[i] if i & CORE_BIT else first[i]) for i in range(size)]))
        return steps
    held = 1
    for bit in [Y_BIT << k for k in range(n_z.bit_length())]:
        steps += [(sent, [(i, i ^ bit) for i in range(size)]) for sent in range(held)]
        held *= 2
    return steps


def owners(size):
    held = [[i] for i in range(size)]
    for sent, pairs in gather_steps(size):
        source = {target: i for i, target in pairs}
        moved = [held[source[i]][sent] for i in range(size)]
        for i in range(size):
            held[i].append(moved[i])
    held = [held[i] + held[i ^ CORE_BIT] for i in range(size)]
    assert all(sorted(row) == list(range(size)) for row in held)
    return held


PAIR_STEPS = ((False, 4, 8), (False, 14, 2), (True, 2, 2), (True, 1, 4))
PAIR_OFFSETS = ((4, 14, 6), (8, 2, 10, 12))

ORDER = {
    "F2": ("S3",),
    "F7": ("K", "F6"),
    "D7": ("P2",),
    "Sx": ("Ox", "F1"),
}
MERGED = False
GROUPS = (4, 3, 1)


class Work:
    def __init__(self, order):
        self.order, self.made, self.makers = order, {}, {}

    def add(self, name, operand, make):
        self.makers[name] = (operand, make)

    def get(self, name):
        if name not in self.made:
            operand, make = self.makers[name]
            value = operand()
            others = [self.get(other) for other in self.order.get(name, ())]
            if others:
                value = lax.optimization_barrier((value, others))[0]
            self.made[name] = make(value)
        return self.made[name]


def share_sims(work, sims, obs, codes, n_row, n_col):
    rows, depth = obs.shape[0], sims.shape[0]

    def add_swap(name, of, axis, size, bit):
        work.add(name, lambda: work.get(of), lambda value: swap(value, axis, size, bit))

    work.add("own", lambda: sims, lambda value: value)
    work.add("obs0", lambda: obs, lambda value: value)
    work.add("codes0", lambda: codes, lambda value: value)
    if (n_row, n_col) != (16, 2):
        names = ["own"]
        for k, (sent, pairs) in enumerate(gather_steps(n_row)):
            names.append(f"S{k + 1}")
            work.add(
                names[-1],
                lambda of=names[sent]: work.get(of),
                lambda value, pairs=pairs: lax.ppermute(value, "row", pairs),
            )
        names += [f"{name}c" for name in names]
        for name in names[n_row // 2 :]:
            add_swap(name, name[:-1], "row", n_row, CORE_BIT)
        for what in ("obs", "codes"):
            names.append(f"{what}0")
            for k in range(1, n_col):
                top = 1 << (k.bit_length() - 1)
                names.append(f"{what}{k}")
                add_swap(names[-1], f"{what}{k ^ top}", "col", n_col, top)
        at = [(k, 0) for k in range(len(names))]
        n = n_row + n_col
        table = [held for held in owners(n_row) for _ in range(n_col)]
        return names, [(a, a) for a in at[:n_row]], at[n_row:n], at[n:], table
    for k, (again, off_a, off_b) in enumerate(PAIR_STEPS):
        pairs = [(2 * r + c, 2 * (r ^ (off_b if c else off_a)) + c) for r in range(n_row) for c in range(2)]
        work.add(
            f"S{k + 1}",
            lambda of="S1" if again else "own": work.get(of),
            lambda value, pairs=pairs: lax.ppermute(value, ("row", "col"), pairs),
        )
    arrived = lambda: [work.get(f"S{k + 1}") for k in range(4)]
    if MERGED:
        work.add("mine", lambda: arrived() + [obs, codes], lambda parts: jnp.concatenate(parts, axis=0))
        obs_at = [(1, 4 * depth), (2, 4 * depth)]
        names = ["own", "mine", "Sx"]
    else:
        work.add("mine", arrived, lambda parts: jnp.concatenate(parts, axis=0))
        work.add("both", lambda: [obs, codes], lambda parts: jnp.concatenate(parts, axis=0))
        add_swap("Ox", "both", "col", n_col, 1)
        names = ["own", "mine", "Sx"]
        obs_at = [(6, 0), (7, 0)]
    add_swap("Sx", "mine", "col", n_col, 1)
    blocks = [((0, 0), (0, 0))]
    for k in range(3):
        blocks += [((1, k * depth),) * 2, ((2, k * depth),) * 2]
    blocks += [((2, 3 * depth), (1, 3 * depth))]
    blocks += [tuple((s + len(names), k) for s, k in block) for block in blocks]
    table = []
    for r in range(n_row):
        for c in range(2):
            here, there = PAIR_OFFSETS[c], PAIR_OFFSETS[1 - c]
            offs = [0] + [o for k in range(3) for o in (here[k], there[k])] + [PAIR_OFFSETS[1][3]]
            table.append([r ^ o for o in offs] + [r ^ CORE_BIT ^ o for o in offs])
            assert sorted(table[-1]) == list(range(n_row))
    for name in tuple(names):
        names.append(f"Sc{name}")
        add_swap(names[-1], name, "row", n_row, CORE_BIT)
    if not MERGED:
        names += ["both", "Ox"]
    return names, blocks, obs_at, [(s, k + rows) for s, k in obs_at], table


def kinds_of_place(n_row, n_col, table):
    held = owners(n_row)
    kind_of, seen = [], []
    for r in range(n_row):
        offsets = [r ^ owner for owner in held[r]]
        kind_of.append([])
        for c in range(n_col):
            what = (offsets, [held[r].index(owner) for owner in table[r * n_col + c]])
            if what not in seen:
                seen.append(what)
            kind_of[-1].append(seen.index(what))
    return kind_of, [w[0] for w in seen], [w[1] for w in seen]


def choose(index, options):
    if all(o == options[0] for o in options):
        return options[0]
    out = jnp.int32(options[0])
    for i, option in enumerate(options[1:], 1):
        out = jnp.where(index == i, option, out)
    return out


def weight_kernel(blocks, obs_at, codes_at, kinds, depth, rows, near, n_in, *refs):
    n_sim, n_piece = len(blocks), len(obs_at)
    arrays, (weight_out, total_out) = refs[:n_in], refs[n_in : n_in + 2]
    obs_scr, low_scr, high_scr, value_scr, square_scr, factor_scr, owner_scr = refs[n_in + 2 :]
    my_row, my_col = lax.axis_index("row"), lax.axis_index("col")
    n_obs = n_piece * rows
    groups = depth // LANES

    kind_of, offsets, places = kinds
    n_col = len(kind_of[0])
    kind = choose(my_row * n_col + my_col, [k for row in kind_of for k in row])
    for b in range(n_sim):
        owner_scr[b] = lax.bitwise_xor(my_row, choose(kind, [o[b] for o in offsets])) * groups

    for i in range(n_piece):
        at = pl.ds(pl.multiple_of(lax.bitwise_xor(my_col, i) * rows, rows), rows)
        (s, k), (t, m) = obs_at[i], codes_at[i]
        obs_scr[at, :] = arrays[s][k : k + rows, :]
        codes = arrays[t][m : m + 2 * near, :rows].astype(jnp.float32).T.astype(jnp.int32)
        pad = jnp.zeros((rows, LANES - near), jnp.int32)
        high_scr[at, :] = jnp.concatenate([codes[:, :near], pad - 1], axis=1)
        low_scr[at, :] = jnp.concatenate([codes[:, near:], pad], axis=1)
    obs = obs_scr[...]
    obs_float = obs.astype(jnp.float32)
    square_scr[...] = jnp.broadcast_to(jnp.sum(obs_float * obs_float, axis=1, keepdims=True), (n_obs, LANES))

    for b, at_cols in enumerate(blocks):
        block, at_one = [arrays[s][k : k + depth, :] for s, k in at_cols]
        if at_cols[0] != at_cols[1]:
            block = jnp.where(my_col == 0, block, at_one)
        squares = block.astype(jnp.float32)
        squares = squares * squares
        folded = squares[:, :LANES]
        for g in range(1, block.shape[1] // LANES):
            folded += squares[:, g * LANES : (g + 1) * LANES]
        sim_square = jnp.sum(folded.T, axis=0, keepdims=True)
        cross = lax.dot_general(obs, block, (((1,), (1,)), ((), ())), preferred_element_type=jnp.float32)
        place = choose(kind, [p[b] for p in places]) * groups
        for g in range(groups):
            at = slice(g * LANES, (g + 1) * LANES)
            value_scr[place + g] = sim_square[:, at] - 2.0 * cross[:, at]

    tile = 8
    some = min(n_obs, 64)

    def add_near(t, carry):
        for r in range(some // tile):
            at = pl.ds(pl.multiple_of(t * some + r * tile, tile), tile)
            low, high = low_scr[at, :], high_scr[at, :]
            total = jnp.zeros((tile, LANES), jnp.float32)
            for c in range(n_sim * groups):
                found = jnp.take_along_axis(value_scr[c, at, :], low, axis=1)
                total += jnp.where(high == owner_scr[c // groups] + c % groups, found, 0.0)
            factor_scr[at, :] = total
        return carry

    lax.fori_loop(0, n_obs // some, add_near, 0)
    width = square_scr[...] + jnp.sum(factor_scr[...], axis=1, keepdims=True) / near + EPSILON
    factor_scr[...] = (-SHARPNESS * math.log2(math.e)) / width
    part = min(n_obs, 32)

    def weigh(t, carry):
        at = pl.ds(pl.multiple_of(t * part, part), part)
        factor, square = factor_scr[at, :], square_scr[at, :]
        total = jnp.zeros((part, LANES), jnp.float32)
        for c in range(n_sim * groups):
            weight = jnp.exp2(factor * (square + value_scr[c, at, :]))
            weight_out[c // groups, at, c % groups * LANES : (c % groups + 1) * LANES] = weight.astype(jnp.bfloat16)
            total += weight
        total_out[at, :] = total
        return carry

    lax.fori_loop(0, n_obs // part, weigh, 0)
    total_out[...] = jnp.broadcast_to(jnp.sum(total_out[...], axis=1, keepdims=True), total_out.shape)


def product_kernel(columns, first, last, weight, *refs):
    blocks, rest, out = refs[: len(columns)], refs[len(columns) : -1], refs[-1]
    so_far = None if first else rest[-1]
    total_ref = rest[0] if last else None
    cells = out.shape[1]
    step = min(cells, 256)
    for j in range(cells // step):
        at = slice(j * step, (j + 1) * step)
        total = None if so_far is None else so_far[:, at]
        for column, block in zip(columns, blocks):
            term = jnp.dot(
                weight[column], block[:, at], preferred_element_type=jnp.float32
            )
            total = term if total is None else total + term
        if total_ref is not None:
            total = total / total_ref[:, :1]
        out[:, at] = total.astype(out.dtype)


def call(kernel, vmem, **kw):
    return pl.pallas_call(kernel, compiler_params=pltpu.CompilerParams(vmem_limit_bytes=vmem << 20), **kw)


def per_device(n_row, n_col, obs_summaries, sim_summaries, neighbours, field):
    f32, bf16 = jnp.float32, jnp.bfloat16
    rows, dims = obs_summaries.shape
    depth, cells = field.shape

    index = neighbours.T
    codes = jnp.concatenate([index // LANES, index % LANES], axis=0).astype(bf16)
    work = Work(ORDER if (n_row, n_col) == (16, 2) else {})
    names, at_blocks, at_obs, at_codes, table = share_sims(work, sim_summaries, obs_summaries, codes, n_row, n_col)
    n_sim, n_obs = n_row, n_col * rows
    kinds = kinds_of_place(n_row, n_col, table)
    weigh = call(
        functools.partial(
            weight_kernel, at_blocks, at_obs, at_codes, kinds, depth, rows, neighbours.shape[1], len(names)
        ),
        40,
        in_specs=[VMEM] * len(names),
        out_specs=[VMEM] * 2,
        out_shape=[
            jax.ShapeDtypeStruct((n_sim, n_obs, depth), bf16),
            jax.ShapeDtypeStruct((n_obs, LANES), f32),
        ],
        scratch_shapes=[
            pltpu.VMEM((n_obs, dims), bf16),
            pltpu.VMEM((n_obs, LANES), jnp.int32),
            pltpu.VMEM((n_obs, LANES), jnp.int32),
            pltpu.VMEM((n_sim * depth // LANES, n_obs, LANES), f32),
            pltpu.VMEM((n_obs, LANES), f32),
            pltpu.VMEM((n_obs, LANES), f32),
            pltpu.SMEM((n_sim,), jnp.int32),
        ],
        cost_estimate=SMALL,
        name="weights",
    )
    work.add("K", lambda: [work.get(name) for name in names], lambda arrays: weigh(*arrays))

    n_half = n_sim // 2
    work.add("F0", lambda: field, lambda value: value)
    for k, (sent, pairs) in enumerate(gather_steps(n_row)):
        work.add(
            f"F{k + 1}",
            lambda sent=sent: work.get(f"F{sent}"),
            lambda value, pairs=pairs: lax.ppermute(value, "row", pairs),
        )
    for k in range(n_half):
        work.add(f"D{k}", lambda k=k: work.get(f"F{k}"), lambda value: swap(value, "row", n_row, CORE_BIT))

    def product(first, last, parts):
        done, (weight, total), before, both = last == n_half, *parts
        columns = [*range(first, last), *range(n_half + first, n_half + last)]
        extra = ([total] if done else []) + ([] if before is None else [before])
        return call(
            functools.partial(product_kernel, columns, before is None, done),
            28,
            in_specs=[VMEM] * (1 + len(both) + len(extra)),
            out_specs=VMEM,
            out_shape=jax.ShapeDtypeStruct((n_obs, cells), bf16 if done else f32),
            cost_estimate=SMALL,
            name="product",
        )(weight, *both, *extra)

    groups = GROUPS if n_half == sum(GROUPS) else (n_half // 2, n_half - n_half // 2 - 1, 1)
    first = 0
    for g, count in enumerate(groups):
        at = range(first, first + count)
        work.add(
            f"P{g + 1}",
            lambda g=g, at=at: (
                work.get("K"),
                work.get(f"P{g}") if g else None,
                [work.get(f"F{k}") for k in at] + [work.get(f"D{k}") for k in at],
            ),
            lambda parts, at=at: product(at.start, at.stop, parts),
        )
        first += count
    return work.get(f"P{len(groups)}")


def solution(mesh):
    return jax.shard_map(
        functools.partial(per_device, mesh.shape["row"], mesh.shape["col"]),
        mesh=mesh,
        in_specs=(
            P(("row", "col"), None),
            P("row", None),
            P(("row", "col"), None),
            P("row", "col"),
        ),
        out_specs=P("row", "col"),
        check_vma=False,
    )
```

```python
import functools
import math

import jax
import jax.numpy as jnp
from jax import lax
from jax.experimental import pallas as pl
from jax.experimental.pallas import tpu as pltpu
from jax.sharding import PartitionSpec as P

SHARPNESS = 32.0
EPSILON = 1e-06
LANES = 128
CORE_BIT = 1
Y_BIT = 2
VMEM = pl.BlockSpec(memory_space=pltpu.VMEM)
SMALL = pl.CostEstimate(flops=1024, bytes_accessed=1024, transcendentals=0)


def swap(value, axis, size, bit):
    return lax.ppermute(value, axis, [(i, i ^ bit) for i in range(size)])


def gather_steps(size):
    n_z = size // 4
    steps = []
    if n_z == 4:
        across = [(i ^ 12) if (i >> 2) in (1, 2) else (i ^ Y_BIT) for i in range(size)]
        inside = [i ^ 4 for i in range(size)]
        for sent, first in ((0, inside), (0, across), (1, across), (2, inside), (3, inside), (4, across), (5, across)):
            second = across if first is inside else inside
            steps.append((sent, [(i, second[i] if i & CORE_BIT else first[i]) for i in range(size)]))
        return steps
    held = 1
    for bit in [Y_BIT << k for k in range(n_z.bit_length())]:
        steps += [(sent, [(i, i ^ bit) for i in range(size)]) for sent in range(held)]
        held *= 2
    return steps


def owners(size):
    held = [[i] for i in range(size)]
    for sent, pairs in gather_steps(size):
        source = {target: i for i, target in pairs}
        moved = [held[source[i]][sent] for i in range(size)]
        for i in range(size):
            held[i].append(moved[i])
    held = [held[i] + held[i ^ CORE_BIT] for i in range(size)]
    assert all(sorted(row) == list(range(size)) for row in held)
    return held


PAIR_STEPS = ((False, 4, 8), (False, 14, 2), (True, 2, 2), (True, 1, 4))
PAIR_OFFSETS = ((4, 14, 6), (8, 2, 10, 12))

ORDER = {
    "F2": ("Ox",),
    "F7": ("K", "F6"),
    "D7": ("P2",),
    "Sx": ("Ox", "F1"),
    "S3": ("S2",),
    "S4": ("S2",),
}
MERGED = False
GROUPS = (4, 3)


class Work:
    def __init__(self, order):
        self.order, self.made, self.makers = order, {}, {}

    def add(self, name, operand, make):
        self.makers[name] = (operand, make)

    def get(self, name):
        if name not in self.made:
            operand, make = self.makers[name]
            value = operand()
            others = [self.get(other) for other in self.order.get(name, ())]
            if others:
                value = lax.optimization_barrier((value, others))[0]
            self.made[name] = make(value)
        return self.made[name]


def share_sims(work, sims, obs, codes, n_row, n_col):
    rows, depth = obs.shape[0], sims.shape[0]

    def add_swap(name, of, axis, size, bit):
        work.add(name, lambda: work.get(of), lambda value: swap(value, axis, size, bit))

    work.add("own", lambda: sims, lambda value: value)
    work.add("obs0", lambda: obs, lambda value: value)
    work.add("codes0", lambda: codes, lambda value: value)
    if (n_row, n_col) != (16, 2):
        names = ["own"]
        for k, (sent, pairs) in enumerate(gather_steps(n_row)):
            names.append(f"S{k + 1}")
            work.add(
                names[-1],
                lambda of=names[sent]: work.get(of),
                lambda value, pairs=pairs: lax.ppermute(value, "row", pairs),
            )
        names += [f"{name}c" for name in names]
        for name in names[n_row // 2 :]:
            add_swap(name, name[:-1], "row", n_row, CORE_BIT)
        for what in ("obs", "codes"):
            names.append(f"{what}0")
            for k in range(1, n_col):
                top = 1 << (k.bit_length() - 1)
                names.append(f"{what}{k}")
                add_swap(names[-1], f"{what}{k ^ top}", "col", n_col, top)
        at = [(k, 0) for k in range(len(names))]
        n = n_row + n_col
        table = [held for held in owners(n_row) for _ in range(n_col)]
        return names, [(a, a) for a in at[:n_row]], at[n_row:n], at[n:], table
    for k, (again, off_a, off_b) in enumerate(PAIR_STEPS):
        pairs = [(2 * r + c, 2 * (r ^ (off_b if c else off_a)) + c) for r in range(n_row) for c in range(2)]
        work.add(
            f"S{k + 1}",
            lambda of="S1" if again else "own": work.get(of),
            lambda value, pairs=pairs: lax.ppermute(value, ("row", "col"), pairs),
        )
    arrived = lambda: [work.get(f"S{k + 1}") for k in range(4)]
    if MERGED:
        work.add("mine", lambda: arrived() + [obs, codes], lambda parts: jnp.concatenate(parts, axis=0))
        obs_at = [(1, 4 * depth), (2, 4 * depth)]
        names = ["own", "mine", "Sx"]
    else:
        work.add("mine", arrived, lambda parts: jnp.concatenate(parts, axis=0))
        work.add("both", lambda: [obs, codes], lambda parts: jnp.concatenate(parts, axis=0))
        add_swap("Ox", "both", "col", n_col, 1)
        names = ["own", "mine", "Sx"]
        obs_at = [(6, 0), (7, 0)]
    add_swap("Sx", "mine", "col", n_col, 1)
    blocks = [((0, 0), (0, 0))]
    for k in range(3):
        blocks += [((1, k * depth),) * 2, ((2, k * depth),) * 2]
    blocks += [((2, 3 * depth), (1, 3 * depth))]
    blocks += [tuple((s + len(names), k) for s, k in block) for block in blocks]
    table = []
    for r in range(n_row):
        for c in range(2):
            here, there = PAIR_OFFSETS[c], PAIR_OFFSETS[1 - c]
            offs = [0] + [o for k in range(3) for o in (here[k], there[k])] + [PAIR_OFFSETS[1][3]]
            table.append([r ^ o for o in offs] + [r ^ CORE_BIT ^ o for o in offs])
            assert sorted(table[-1]) == list(range(n_row))
    for name in tuple(names):
        names.append(f"Sc{name}")
        add_swap(names[-1], name, "row", n_row, CORE_BIT)
    if not MERGED:
        names += ["both", "Ox"]
    return names, blocks, obs_at, [(s, k + rows) for s, k in obs_at], table


def kinds_of_place(n_row, n_col, table):
    held = owners(n_row)
    kind_of, seen = [], []
    for r in range(n_row):
        offsets = [r ^ owner for owner in held[r]]
        kind_of.append([])
        for c in range(n_col):
            what = (offsets, [held[r].index(owner) for owner in table[r * n_col + c]])
            if what not in seen:
                seen.append(what)
            kind_of[-1].append(seen.index(what))
    return kind_of, [w[0] for w in seen], [w[1] for w in seen]


def choose(index, options):
    if all(o == options[0] for o in options):
        return options[0]
    out = jnp.int32(options[0])
    for i, option in enumerate(options[1:], 1):
        out = jnp.where(index == i, option, out)
    return out


def weight_kernel(blocks, obs_at, codes_at, kinds, depth, rows, near, n_in, *refs):
    n_sim, n_piece = len(blocks), len(obs_at)
    arrays, (weight_out, total_out) = refs[:n_in], refs[n_in : n_in + 2]
    obs_scr, low_scr, high_scr, value_scr, square_scr, factor_scr, owner_scr = refs[n_in + 2 :]
    my_row, my_col = lax.axis_index("row"), lax.axis_index("col")
    n_obs = n_piece * rows
    groups = depth // LANES

    kind_of, offsets, places = kinds
    n_col = len(kind_of[0])
    kind = choose(my_row * n_col + my_col, [k for row in kind_of for k in row])
    for b in range(n_sim):
        owner_scr[b] = lax.bitwise_xor(my_row, choose(kind, [o[b] for o in offsets])) * groups

    for i in range(n_piece):
        at = pl.ds(pl.multiple_of(lax.bitwise_xor(my_col, i) * rows, rows), rows)
        (s, k), (t, m) = obs_at[i], codes_at[i]
        obs_scr[at, :] = arrays[s][k : k + rows, :]
        codes = arrays[t][m : m + 2 * near, :rows].astype(jnp.float32).T.astype(jnp.int32)
        pad = jnp.zeros((rows, LANES - near), jnp.int32)
        high_scr[at, :] = jnp.concatenate([codes[:, :near], pad - 1], axis=1)
        low_scr[at, :] = jnp.concatenate([codes[:, near:], pad], axis=1)
    obs = obs_scr[...]
    obs_float = obs.astype(jnp.float32)
    square_scr[...] = jnp.broadcast_to(jnp.sum(obs_float * obs_float, axis=1, keepdims=True), (n_obs, LANES))

    for b, at_cols in enumerate(blocks):
        block, at_one = [arrays[s][k : k + depth, :] for s, k in at_cols]
        if at_cols[0] != at_cols[1]:
            block = jnp.where(my_col == 0, block, at_one)
        squares = block.astype(jnp.float32)
        squares = squares * squares
        folded = squares[:, :LANES]
        for g in range(1, block.shape[1] // LANES):
            folded += squares[:, g * LANES : (g + 1) * LANES]
        sim_square = jnp.sum(folded.T, axis=0, keepdims=True)
        cross = lax.dot_general(obs, block, (((1,), (1,)), ((), ())), preferred_element_type=jnp.float32)
        place = choose(kind, [p[b] for p in places]) * groups
        for g in range(groups):
            at = slice(g * LANES, (g + 1) * LANES)
            value_scr[place + g] = sim_square[:, at] - 2.0 * cross[:, at]

    tile = 8
    some = min(n_obs, 64)

    def add_near(t, carry):
        for r in range(some // tile):
            at = pl.ds(pl.multiple_of(t * some + r * tile, tile), tile)
            low, high = low_scr[at, :], high_scr[at, :]
            total = jnp.zeros((tile, LANES), jnp.float32)
            for c in range(n_sim * groups):
                found = jnp.take_along_axis(value_scr[c, at, :], low, axis=1)
                total += jnp.where(high == owner_scr[c // groups] + c % groups, found, 0.0)
            factor_scr[at, :] = total
        return carry

    lax.fori_loop(0, n_obs // some, add_near, 0)
    width = square_scr[...] + jnp.sum(factor_scr[...], axis=1, keepdims=True) / near + EPSILON
    factor_scr[...] = (-SHARPNESS * math.log2(math.e)) / width
    part = min(n_obs, 32)

    def weigh(t, carry):
        at = pl.ds(pl.multiple_of(t * part, part), part)
        factor, square = factor_scr[at, :], square_scr[at, :]
        total = jnp.zeros((part, LANES), jnp.float32)
        for c in range(n_sim * groups):
            weight = jnp.exp2(factor * (square + value_scr[c, at, :]))
            weight_out[c // groups, at, c % groups * LANES : (c % groups + 1) * LANES] = weight.astype(jnp.bfloat16)
            total += weight
        total_out[at, :] = total
        return carry

    lax.fori_loop(0, n_obs // part, weigh, 0)
    total_out[...] = jnp.broadcast_to(jnp.sum(total_out[...], axis=1, keepdims=True), total_out.shape)


def product_kernel(columns, first, last, weight, *refs):
    blocks, rest, out = refs[: len(columns)], refs[len(columns) : -1], refs[-1]
    so_far = None if first else rest[-1]
    total_ref = rest[0] if last else None
    cells = out.shape[1]
    step = min(cells, 256)
    for j in range(cells // step):
        at = slice(j * step, (j + 1) * step)
        total = None if so_far is None else so_far[:, at]
        for column, block in zip(columns, blocks):
            term = jnp.dot(
                weight[column], block[:, at], preferred_element_type=jnp.float32
            )
            total = term if total is None else total + term
        if total_ref is not None:
            total = total / total_ref[:, :1]
        out[:, at] = total.astype(out.dtype)


def call(kernel, vmem, **kw):
    return pl.pallas_call(kernel, compiler_params=pltpu.CompilerParams(vmem_limit_bytes=vmem << 20), **kw)


def per_device(n_row, n_col, obs_summaries, sim_summaries, neighbours, field):
    f32, bf16 = jnp.float32, jnp.bfloat16
    rows, dims = obs_summaries.shape
    depth, cells = field.shape

    index = neighbours.T
    codes = jnp.concatenate([index // LANES, index % LANES], axis=0).astype(bf16)
    work = Work(ORDER if (n_row, n_col) == (16, 2) else {})
    names, at_blocks, at_obs, at_codes, table = share_sims(work, sim_summaries, obs_summaries, codes, n_row, n_col)
    n_sim, n_obs = n_row, n_col * rows
    kinds = kinds_of_place(n_row, n_col, table)
    weigh = call(
        functools.partial(
            weight_kernel, at_blocks, at_obs, at_codes, kinds, depth, rows, neighbours.shape[1], len(names)
        ),
        40,
        in_specs=[VMEM] * len(names),
        out_specs=[VMEM] * 2,
        out_shape=[
            jax.ShapeDtypeStruct((n_sim, n_obs, depth), bf16),
            jax.ShapeDtypeStruct((n_obs, LANES), f32),
        ],
        scratch_shapes=[
            pltpu.VMEM((n_obs, dims), bf16),
            pltpu.VMEM((n_obs, LANES), jnp.int32),
            pltpu.VMEM((n_obs, LANES), jnp.int32),
            pltpu.VMEM((n_sim * depth // LANES, n_obs, LANES), f32),
            pltpu.VMEM((n_obs, LANES), f32),
            pltpu.VMEM((n_obs, LANES), f32),
            pltpu.SMEM((n_sim,), jnp.int32),
        ],
        cost_estimate=SMALL,
        name="weights",
    )
    work.add("K", lambda: [work.get(name) for name in names], lambda arrays: weigh(*arrays))

    n_half = n_sim // 2
    work.add("F0", lambda: field, lambda value: value)
    for k, (sent, pairs) in enumerate(gather_steps(n_row)):
        work.add(
            f"F{k + 1}",
            lambda sent=sent: work.get(f"F{sent}"),
            lambda value, pairs=pairs: lax.ppermute(value, "row", pairs),
        )
    for k in range(n_half):
        work.add(f"D{k}", lambda k=k: work.get(f"F{k}"), lambda value: swap(value, "row", n_row, CORE_BIT))

    def product(columns, done, parts):
        (weight, total), before, held = parts
        extra = ([total] if done else []) + ([] if before is None else [before])
        return call(
            functools.partial(product_kernel, columns, before is None, done),
            28,
            in_specs=[VMEM] * (1 + len(held) + len(extra)),
            out_specs=VMEM,
            out_shape=jax.ShapeDtypeStruct((n_obs, cells), bf16 if done else f32),
            cost_estimate=SMALL,
            name="product",
        )(weight, *held, *extra)

    groups = GROUPS if n_half == sum(GROUPS) + 1 else (n_half // 2, n_half - n_half // 2 - 1)
    ends = [sum(groups[:g]) for g in range(len(groups) + 1)]
    groups = [[f"{what}{k}" for what in "FD" for k in range(*at)] for at in zip(ends[:-1], ends[1:])]
    groups += [[f"F{n_half - 1}"], [f"D{n_half - 1}"]]
    for g, group in enumerate(groups):
        columns = [int(name[1:]) + (n_half if name[0] == "D" else 0) for name in group]
        work.add(
            f"P{g + 1}",
            lambda g=g, group=group: (
                work.get("K"),
                work.get(f"P{g}") if g else None,
                [work.get(name) for name in group],
            ),
            lambda parts, columns=columns, done=g == len(groups) - 1: product(columns, done, parts),
        )
    return work.get(f"P{len(groups)}")


def solution(mesh):
    return jax.shard_map(
        functools.partial(per_device, mesh.shape["row"], mesh.shape["col"]),
        mesh=mesh,
        in_specs=(
            P(("row", "col"), None),
            P("row", None),
            P(("row", "col"), None),
            P("row", "col"),
        ),
        out_specs=P("row", "col"),
        check_vma=False,
    )
```

```python
import functools
import math

import jax
import jax.numpy as jnp
from jax import lax
from jax.experimental import pallas as pl
from jax.experimental.pallas import tpu as pltpu
from jax.sharding import PartitionSpec as P

SHARPNESS = 32.0
EPSILON = 1e-06
LANES = 128
CORE_BIT = 1
Y_BIT = 2
VMEM = pl.BlockSpec(memory_space=pltpu.VMEM)
SMALL = pl.CostEstimate(flops=1024, bytes_accessed=1024, transcendentals=0)


def swap(value, axis, size, bit):
    return lax.ppermute(value, axis, [(i, i ^ bit) for i in range(size)])


def gather_steps(size):
    n_z = size // 4
    steps = []
    if n_z == 4:
        across = [(i ^ 12) if (i >> 2) in (1, 2) else (i ^ Y_BIT) for i in range(size)]
        inside = [i ^ 4 for i in range(size)]
        for sent, first in ((0, inside), (0, across), (1, across), (2, inside), (3, inside), (4, across), (5, across)):
            second = across if first is inside else inside
            steps.append((sent, [(i, second[i] if i & CORE_BIT else first[i]) for i in range(size)]))
        return steps
    held = 1
    for bit in [Y_BIT << k for k in range(n_z.bit_length())]:
        steps += [(sent, [(i, i ^ bit) for i in range(size)]) for sent in range(held)]
        held *= 2
    return steps


def owners(size):
    held = [[i] for i in range(size)]
    for sent, pairs in gather_steps(size):
        source = {target: i for i, target in pairs}
        moved = [held[source[i]][sent] for i in range(size)]
        for i in range(size):
            held[i].append(moved[i])
    held = [held[i] + held[i ^ CORE_BIT] for i in range(size)]
    assert all(sorted(row) == list(range(size)) for row in held)
    return held


PAIR_STEPS = ((False, 4, 8), (False, 1, 2), (True, 2, 2), (True, 10, 4))
PAIR_OFFSETS = ((4, None, 6, 14), (8, 2, 10, 12))
SPARE = 1

ORDER = {
    "F2": ("Ox",),
    "F7": ("K", "F6"),
    "D7": ("P2",),
    "Sx": ("Ox", "F1"),
}
MERGED = False
GROUPS = (4, 3)


class Work:
    def __init__(self, order):
        self.order, self.made, self.makers = order, {}, {}

    def add(self, name, operand, make):
        self.makers[name] = (operand, make)

    def get(self, name):
        if name not in self.made:
            operand, make = self.makers[name]
            value = operand()
            others = [self.get(other) for other in self.order.get(name, ())]
            if others:
                value = lax.optimization_barrier((value, others))[0]
            self.made[name] = make(value)
        return self.made[name]


def share_sims(work, sims, obs, codes, n_row, n_col):
    rows, depth = obs.shape[0], sims.shape[0]

    def add_swap(name, of, axis, size, bit):
        work.add(name, lambda: work.get(of), lambda value: swap(value, axis, size, bit))

    work.add("own", lambda: sims, lambda value: value)
    work.add("obs0", lambda: obs, lambda value: value)
    work.add("codes0", lambda: codes, lambda value: value)
    if (n_row, n_col) != (16, 2):
        names = ["own"]
        for k, (sent, pairs) in enumerate(gather_steps(n_row)):
            names.append(f"S{k + 1}")
            work.add(
                names[-1],
                lambda of=names[sent]: work.get(of),
                lambda value, pairs=pairs: lax.ppermute(value, "row", pairs),
            )
        names += [f"{name}c" for name in names]
        for name in names[n_row // 2 :]:
            add_swap(name, name[:-1], "row", n_row, CORE_BIT)
        for what in ("obs", "codes"):
            names.append(f"{what}0")
            for k in range(1, n_col):
                top = 1 << (k.bit_length() - 1)
                names.append(f"{what}{k}")
                add_swap(names[-1], f"{what}{k ^ top}", "col", n_col, top)
        at = [(k, 0) for k in range(len(names))]
        n = n_row + n_col
        table = [held for held in owners(n_row) for _ in range(n_col)]
        return names, [(a, a) for a in at[:n_row]], at[n_row:n], at[n:], table
    for k, (again, off_a, off_b) in enumerate(PAIR_STEPS):
        pairs = [(2 * r + c, 2 * (r ^ (off_b if c else off_a)) + c) for r in range(n_row) for c in range(2)]
        work.add(
            f"S{k + 1}",
            lambda of="S1" if again else "own": work.get(of),
            lambda value, pairs=pairs: lax.ppermute(value, ("row", "col"), pairs),
        )
    arrived = lambda: [work.get(f"S{k + 1}") for k in range(4)]
    if MERGED:
        work.add("mine", lambda: arrived() + [obs, codes], lambda parts: jnp.concatenate(parts, axis=0))
        obs_at = [(1, 4 * depth), (2, 4 * depth)]
        names = ["own", "mine", "Sx"]
    else:
        work.add("mine", arrived, lambda parts: jnp.concatenate(parts, axis=0))
        work.add("both", lambda: [obs, codes], lambda parts: jnp.concatenate(parts, axis=0))
        add_swap("Ox", "both", "col", n_col, 1)
        names = ["own", "mine", "Sx"]
        obs_at = [(6, 0), (7, 0)]
    add_swap("Sx", "mine", "col", n_col, 1)
    blocks = [((0, 0), (0, 0))]
    kept = [k for k in range(4) if k != SPARE]
    for k in kept:
        blocks += [((1, k * depth),) * 2, ((2, k * depth),) * 2]
    blocks += [((2, SPARE * depth), (1, SPARE * depth))]
    blocks += [tuple((s + len(names), k) for s, k in block) for block in blocks]
    table = []
    for r in range(n_row):
        for c in range(2):
            here, there = PAIR_OFFSETS[c], PAIR_OFFSETS[1 - c]
            offs = [0] + [o for k in kept for o in (here[k], there[k])] + [PAIR_OFFSETS[1][SPARE]]
            table.append([r ^ o for o in offs] + [r ^ CORE_BIT ^ o for o in offs])
            assert sorted(table[-1]) == list(range(n_row))
    for name in tuple(names):
        names.append(f"Sc{name}")
        add_swap(names[-1], name, "row", n_row, CORE_BIT)
    if not MERGED:
        names += ["both", "Ox"]
    return names, blocks, obs_at, [(s, k + rows) for s, k in obs_at], table


def kinds_of_place(n_row, n_col, table):
    held = owners(n_row)
    kind_of, seen = [], []
    for r in range(n_row):
        offsets = [r ^ owner for owner in held[r]]
        kind_of.append([])
        for c in range(n_col):
            what = (offsets, [held[r].index(owner) for owner in table[r * n_col + c]])
            if what not in seen:
                seen.append(what)
            kind_of[-1].append(seen.index(what))
    return kind_of, [w[0] for w in seen], [w[1] for w in seen]


def choose(index, options):
    if all(o == options[0] for o in options):
        return options[0]
    out = jnp.int32(options[0])
    for i, option in enumerate(options[1:], 1):
        out = jnp.where(index == i, option, out)
    return out


def weight_kernel(blocks, obs_at, codes_at, kinds, depth, rows, near, n_in, *refs):
    n_sim, n_piece = len(blocks), len(obs_at)
    arrays, (weight_out, total_out) = refs[:n_in], refs[n_in : n_in + 2]
    obs_scr, low_scr, high_scr, value_scr, square_scr, factor_scr, owner_scr = refs[n_in + 2 :]
    my_row, my_col = lax.axis_index("row"), lax.axis_index("col")
    n_obs = n_piece * rows
    groups = depth // LANES

    kind_of, offsets, places = kinds
    n_col = len(kind_of[0])
    kind = choose(my_row * n_col + my_col, [k for row in kind_of for k in row])
    for b in range(n_sim):
        owner_scr[b] = lax.bitwise_xor(my_row, choose(kind, [o[b] for o in offsets])) * groups

    for i in range(n_piece):
        at = pl.ds(pl.multiple_of(lax.bitwise_xor(my_col, i) * rows, rows), rows)
        (s, k), (t, m) = obs_at[i], codes_at[i]
        obs_scr[at, :] = arrays[s][k : k + rows, :]
        codes = arrays[t][m : m + 2 * near, :rows].astype(jnp.float32).T.astype(jnp.int32)
        pad = jnp.zeros((rows, LANES - near), jnp.int32)
        high_scr[at, :] = jnp.concatenate([codes[:, :near], pad - 1], axis=1)
        low_scr[at, :] = jnp.concatenate([codes[:, near:], pad], axis=1)
    obs = obs_scr[...]
    obs_float = obs.astype(jnp.float32)
    square_scr[...] = jnp.broadcast_to(jnp.sum(obs_float * obs_float, axis=1, keepdims=True), (n_obs, LANES))

    for b, at_cols in enumerate(blocks):
        block, at_one = [arrays[s][k : k + depth, :] for s, k in at_cols]
        if at_cols[0] != at_cols[1]:
            block = jnp.where(my_col == 0, block, at_one)
        squares = block.astype(jnp.float32)
        squares = squares * squares
        folded = squares[:, :LANES]
        for g in range(1, block.shape[1] // LANES):
            folded += squares[:, g * LANES : (g + 1) * LANES]
        sim_square = jnp.sum(folded.T, axis=0, keepdims=True)
        cross = lax.dot_general(obs, block, (((1,), (1,)), ((), ())), preferred_element_type=jnp.float32)
        place = choose(kind, [p[b] for p in places]) * groups
        for g in range(groups):
            at = slice(g * LANES, (g + 1) * LANES)
            value_scr[place + g] = sim_square[:, at] - 2.0 * cross[:, at]

    tile = 8
    some = min(n_obs, 64)

    def add_near(t, carry):
        for r in range(some // tile):
            at = pl.ds(pl.multiple_of(t * some + r * tile, tile), tile)
            low, high = low_scr[at, :], high_scr[at, :]
            total = jnp.zeros((tile, LANES), jnp.float32)
            for c in range(n_sim * groups):
                found = jnp.take_along_axis(value_scr[c, at, :], low, axis=1)
                total += jnp.where(high == owner_scr[c // groups] + c % groups, found, 0.0)
            factor_scr[at, :] = total
        return carry

    lax.fori_loop(0, n_obs // some, add_near, 0)
    width = square_scr[...] + jnp.sum(factor_scr[...], axis=1, keepdims=True) / near + EPSILON
    factor_scr[...] = (-SHARPNESS * math.log2(math.e)) / width
    part = min(n_obs, 32)

    def weigh(t, carry):
        at = pl.ds(pl.multiple_of(t * part, part), part)
        factor, square = factor_scr[at, :], square_scr[at, :]
        total = jnp.zeros((part, LANES), jnp.float32)
        for c in range(n_sim * groups):
            weight = jnp.exp2(factor * (square + value_scr[c, at, :]))
            weight_out[c // groups, at, c % groups * LANES : (c % groups + 1) * LANES] = weight.astype(jnp.bfloat16)
            total += weight
        total_out[at, :] = total
        return carry

    lax.fori_loop(0, n_obs // part, weigh, 0)
    total_out[...] = jnp.broadcast_to(jnp.sum(total_out[...], axis=1, keepdims=True), total_out.shape)


def product_kernel(columns, first, last, weight, *refs):
    blocks, rest, out = refs[: len(columns)], refs[len(columns) : -1], refs[-1]
    so_far = None if first else rest[-1]
    total_ref = rest[0] if last else None
    cells = out.shape[1]
    step = min(cells, 256)
    for j in range(cells // step):
        at = slice(j * step, (j + 1) * step)
        total = None if so_far is None else so_far[:, at]
        for column, block in zip(columns, blocks):
            term = jnp.dot(
                weight[column], block[:, at], preferred_element_type=jnp.float32
            )
            total = term if total is None else total + term
        if total_ref is not None:
            total = total / total_ref[:, :1]
        out[:, at] = total.astype(out.dtype)


def call(kernel, vmem, **kw):
    return pl.pallas_call(kernel, compiler_params=pltpu.CompilerParams(vmem_limit_bytes=vmem << 20), **kw)


def per_device(n_row, n_col, obs_summaries, sim_summaries, neighbours, field):
    f32, bf16 = jnp.float32, jnp.bfloat16
    rows, dims = obs_summaries.shape
    depth, cells = field.shape

    index = neighbours.T
    codes = jnp.concatenate([index // LANES, index % LANES], axis=0).astype(bf16)
    work = Work(ORDER if (n_row, n_col) == (16, 2) else {})
    names, at_blocks, at_obs, at_codes, table = share_sims(work, sim_summaries, obs_summaries, codes, n_row, n_col)
    n_sim, n_obs = n_row, n_col * rows
    kinds = kinds_of_place(n_row, n_col, table)
    weigh = call(
        functools.partial(
            weight_kernel, at_blocks, at_obs, at_codes, kinds, depth, rows, neighbours.shape[1], len(names)
        ),
        40,
        in_specs=[VMEM] * len(names),
        out_specs=[VMEM] * 2,
        out_shape=[
            jax.ShapeDtypeStruct((n_sim, n_obs, depth), bf16),
            jax.ShapeDtypeStruct((n_obs, LANES), f32),
        ],
        scratch_shapes=[
            pltpu.VMEM((n_obs, dims), bf16),
            pltpu.VMEM((n_obs, LANES), jnp.int32),
            pltpu.VMEM((n_obs, LANES), jnp.int32),
            pltpu.VMEM((n_sim * depth // LANES, n_obs, LANES), f32),
            pltpu.VMEM((n_obs, LANES), f32),
            pltpu.VMEM((n_obs, LANES), f32),
            pltpu.SMEM((n_sim,), jnp.int32),
        ],
        cost_estimate=SMALL,
        name="weights",
    )
    work.add("K", lambda: [work.get(name) for name in names], lambda arrays: weigh(*arrays))

    n_half = n_sim // 2
    work.add("F0", lambda: field, lambda value: value)
    for k, (sent, pairs) in enumerate(gather_steps(n_row)):
        work.add(
            f"F{k + 1}",
            lambda sent=sent: work.get(f"F{sent}"),
            lambda value, pairs=pairs: lax.ppermute(value, "row", pairs),
        )
    for k in range(n_half):
        work.add(f"D{k}", lambda k=k: work.get(f"F{k}"), lambda value: swap(value, "row", n_row, CORE_BIT))

    def product(columns, done, parts):
        (weight, total), before, held = parts
        extra = ([total] if done else []) + ([] if before is None else [before])
        return call(
            functools.partial(product_kernel, columns, before is None, done),
            28,
            in_specs=[VMEM] * (1 + len(held) + len(extra)),
            out_specs=VMEM,
            out_shape=jax.ShapeDtypeStruct((n_obs, cells), bf16 if done else f32),
            cost_estimate=SMALL,
            name="product",
        )(weight, *held, *extra)

    groups = GROUPS if n_half == sum(GROUPS) + 1 else (n_half // 2, n_half - n_half // 2 - 1)
    ends = [sum(groups[:g]) for g in range(len(groups) + 1)]
    groups = [[f"{what}{k}" for what in "FD" for k in range(*at)] for at in zip(ends[:-1], ends[1:])]
    groups += [[f"F{n_half - 1}"], [f"D{n_half - 1}"]]
    for g, group in enumerate(groups):
        columns = [int(name[1:]) + (n_half if name[0] == "D" else 0) for name in group]
        work.add(
            f"P{g + 1}",
            lambda g=g, group=group: (
                work.get("K"),
                work.get(f"P{g}") if g else None,
                [work.get(name) for name in group],
            ),
            lambda parts, columns=columns, done=g == len(groups) - 1: product(columns, done, parts),
        )
    return work.get(f"P{len(groups)}")


def solution(mesh):
    return jax.shard_map(
        functools.partial(per_device, mesh.shape["row"], mesh.shape["col"]),
        mesh=mesh,
        in_specs=(
            P(("row", "col"), None),
            P("row", None),
            P(("row", "col"), None),
            P("row", "col"),
        ),
        out_specs=P("row", "col"),
        check_vma=False,
    )
```

```python
import functools
import math

import jax
import jax.numpy as jnp
from jax import lax
from jax.experimental import pallas as pl
from jax.experimental.pallas import tpu as pltpu
from jax.sharding import PartitionSpec as P

SHARPNESS = 32.0
EPSILON = 1e-06
LANES = 128
CORE_BIT = 1
Y_BIT = 2
VMEM = pl.BlockSpec(memory_space=pltpu.VMEM)
SMALL = pl.CostEstimate(flops=1024, bytes_accessed=1024, transcendentals=0)


def swap(value, axis, size, bit):
    return lax.ppermute(value, axis, [(i, i ^ bit) for i in range(size)])


def gather_steps(size):
    n_z = size // 4
    steps = []
    if n_z == 4:
        across = [(i ^ 12) if (i >> 2) in (1, 2) else (i ^ Y_BIT) for i in range(size)]
        inside = [i ^ 4 for i in range(size)]
        for sent, first in ((0, inside), (0, across), (1, across), (2, inside), (3, inside), (4, across), (5, across)):
            second = across if first is inside else inside
            steps.append((sent, [(i, second[i] if i & CORE_BIT else first[i]) for i in range(size)]))
        return steps
    held = 1
    for bit in [Y_BIT << k for k in range(n_z.bit_length())]:
        steps += [(sent, [(i, i ^ bit) for i in range(size)]) for sent in range(held)]
        held *= 2
    return steps


def owners(size):
    held = [[i] for i in range(size)]
    for sent, pairs in gather_steps(size):
        source = {target: i for i, target in pairs}
        moved = [held[source[i]][sent] for i in range(size)]
        for i in range(size):
            held[i].append(moved[i])
    held = [held[i] + held[i ^ CORE_BIT] for i in range(size)]
    assert all(sorted(row) == list(range(size)) for row in held)
    return held


PAIR_STEPS = ((False, 4, 8), (False, 1, 2), (True, 2, 2), (True, 10, 4))
PAIR_OFFSETS = ((4, None, 6, 14), (8, 2, 10, 12))
SPARE = 1

ORDER = {
    "F2": ("Ox",),
    "F3": ("S4",),
    "F7": ("K", "F6"),
    "D7": ("P2",),
    "Sx": ("Ox", "F1"),
}
MERGED = False
GROUPS = (4, 3)


class Work:
    def __init__(self, order):
        self.order, self.made, self.makers = order, {}, {}

    def add(self, name, operand, make):
        self.makers[name] = (operand, make)

    def get(self, name):
        if name not in self.made:
            operand, make = self.makers[name]
            value = operand()
            others = [self.get(other) for other in self.order.get(name, ())]
            if others:
                value = lax.optimization_barrier((value, others))[0]
            self.made[name] = make(value)
        return self.made[name]


def share_sims(work, sims, obs, codes, n_row, n_col):
    rows, depth = obs.shape[0], sims.shape[0]

    def add_swap(name, of, axis, size, bit):
        work.add(name, lambda: work.get(of), lambda value: swap(value, axis, size, bit))

    work.add("own", lambda: sims, lambda value: value)
    work.add("obs0", lambda: obs, lambda value: value)
    work.add("codes0", lambda: codes, lambda value: value)
    if (n_row, n_col) != (16, 2):
        names = ["own"]
        for k, (sent, pairs) in enumerate(gather_steps(n_row)):
            names.append(f"S{k + 1}")
            work.add(
                names[-1],
                lambda of=names[sent]: work.get(of),
                lambda value, pairs=pairs: lax.ppermute(value, "row", pairs),
            )
        names += [f"{name}c" for name in names]
        for name in names[n_row // 2 :]:
            add_swap(name, name[:-1], "row", n_row, CORE_BIT)
        for what in ("obs", "codes"):
            names.append(f"{what}0")
            for k in range(1, n_col):
                top = 1 << (k.bit_length() - 1)
                names.append(f"{what}{k}")
                add_swap(names[-1], f"{what}{k ^ top}", "col", n_col, top)
        at = [(k, 0) for k in range(len(names))]
        n = n_row + n_col
        table = [held for held in owners(n_row) for _ in range(n_col)]
        return names, [(a, a) for a in at[:n_row]], at[n_row:n], at[n:], table
    for k, (again, off_a, off_b) in enumerate(PAIR_STEPS):
        pairs = [(2 * r + c, 2 * (r ^ (off_b if c else off_a)) + c) for r in range(n_row) for c in range(2)]
        work.add(
            f"S{k + 1}",
            lambda of="S1" if again else "own": work.get(of),
            lambda value, pairs=pairs: lax.ppermute(value, ("row", "col"), pairs),
        )
    arrived = lambda: [work.get(f"S{k + 1}") for k in range(4)]
    if MERGED:
        work.add("mine", lambda: arrived() + [obs, codes], lambda parts: jnp.concatenate(parts, axis=0))
        obs_at = [(1, 4 * depth), (2, 4 * depth)]
        names = ["own", "mine", "Sx"]
    else:
        work.add("mine", arrived, lambda parts: jnp.concatenate(parts, axis=0))
        work.add("both", lambda: [obs, codes], lambda parts: jnp.concatenate(parts, axis=0))
        add_swap("Ox", "both", "col", n_col, 1)
        names = ["own", "mine", "Sx"]
        obs_at = [(6, 0), (7, 0)]
    add_swap("Sx", "mine", "col", n_col, 1)
    blocks = [((0, 0), (0, 0))]
    kept = [k for k in range(4) if k != SPARE]
    for k in kept:
        blocks += [((1, k * depth),) * 2, ((2, k * depth),) * 2]
    blocks += [((2, SPARE * depth), (1, SPARE * depth))]
    blocks += [tuple((s + len(names), k) for s, k in block) for block in blocks]
    table = []
    for r in range(n_row):
        for c in range(2):
            here, there = PAIR_OFFSETS[c], PAIR_OFFSETS[1 - c]
            offs = [0] + [o for k in kept for o in (here[k], there[k])] + [PAIR_OFFSETS[1][SPARE]]
            table.append([r ^ o for o in offs] + [r ^ CORE_BIT ^ o for o in offs])
            assert sorted(table[-1]) == list(range(n_row))
    for name in tuple(names):
        names.append(f"Sc{name}")
        add_swap(names[-1], name, "row", n_row, CORE_BIT)
    if not MERGED:
        names += ["both", "Ox"]
    return names, blocks, obs_at, [(s, k + rows) for s, k in obs_at], table


def kinds_of_place(n_row, n_col, table):
    held = owners(n_row)
    kind_of, seen = [], []
    for r in range(n_row):
        offsets = [r ^ owner for owner in held[r]]
        kind_of.append([])
        for c in range(n_col):
            what = (offsets, [held[r].index(owner) for owner in table[r * n_col + c]])
            if what not in seen:
                seen.append(what)
            kind_of[-1].append(seen.index(what))
    return kind_of, [w[0] for w in seen], [w[1] for w in seen]


def choose(index, options):
    if all(o == options[0] for o in options):
        return options[0]
    out = jnp.int32(options[0])
    for i, option in enumerate(options[1:], 1):
        out = jnp.where(index == i, option, out)
    return out


def weight_kernel(blocks, obs_at, codes_at, kinds, depth, rows, near, n_in, *refs):
    n_sim, n_piece = len(blocks), len(obs_at)
    arrays, (weight_out, total_out) = refs[:n_in], refs[n_in : n_in + 2]
    obs_scr, low_scr, high_scr, value_scr, square_scr, factor_scr, owner_scr = refs[n_in + 2 :]
    my_row, my_col = lax.axis_index("row"), lax.axis_index("col")
    n_obs = n_piece * rows
    groups = depth // LANES

    kind_of, offsets, places = kinds
    n_col = len(kind_of[0])
    kind = choose(my_row * n_col + my_col, [k for row in kind_of for k in row])
    for b in range(n_sim):
        owner_scr[b] = lax.bitwise_xor(my_row, choose(kind, [o[b] for o in offsets])) * groups

    for i in range(n_piece):
        at = pl.ds(pl.multiple_of(lax.bitwise_xor(my_col, i) * rows, rows), rows)
        (s, k), (t, m) = obs_at[i], codes_at[i]
        obs_scr[at, :] = arrays[s][k : k + rows, :]
        codes = arrays[t][m : m + 2 * near, :rows].astype(jnp.float32).T.astype(jnp.int32)
        pad = jnp.zeros((rows, LANES - near), jnp.int32)
        high_scr[at, :] = jnp.concatenate([codes[:, :near], pad - 1], axis=1)
        low_scr[at, :] = jnp.concatenate([codes[:, near:], pad], axis=1)
    obs = obs_scr[...]
    obs_float = obs.astype(jnp.float32)
    square_scr[...] = jnp.broadcast_to(jnp.sum(obs_float * obs_float, axis=1, keepdims=True), (n_obs, LANES))

    for b, at_cols in enumerate(blocks):
        block, at_one = [arrays[s][k : k + depth, :] for s, k in at_cols]
        if at_cols[0] != at_cols[1]:
            block = jnp.where(my_col == 0, block, at_one)
        squares = block.astype(jnp.float32)
        squares = squares * squares
        folded = squares[:, :LANES]
        for g in range(1, block.shape[1] // LANES):
            folded += squares[:, g * LANES : (g + 1) * LANES]
        sim_square = jnp.sum(folded.T, axis=0, keepdims=True)
        cross = lax.dot_general(obs, block, (((1,), (1,)), ((), ())), preferred_element_type=jnp.float32)
        place = choose(kind, [p[b] for p in places]) * groups
        for g in range(groups):
            at = slice(g * LANES, (g + 1) * LANES)
            value_scr[place + g] = sim_square[:, at] - 2.0 * cross[:, at]

    tile = 8
    some = min(n_obs, 64)

    def add_near(t, carry):
        for r in range(some // tile):
            at = pl.ds(pl.multiple_of(t * some + r * tile, tile), tile)
            low, high = low_scr[at, :], high_scr[at, :]
            total = jnp.zeros((tile, LANES), jnp.float32)
            for c in range(n_sim * groups):
                found = jnp.take_along_axis(value_scr[c, at, :], low, axis=1)
                total += jnp.where(high == owner_scr[c // groups] + c % groups, found, 0.0)
            factor_scr[at, :] = total
        return carry

    lax.fori_loop(0, n_obs // some, add_near, 0)
    width = square_scr[...] + jnp.sum(factor_scr[...], axis=1, keepdims=True) / near + EPSILON
    factor_scr[...] = (-SHARPNESS * math.log2(math.e)) / width
    part = min(n_obs, 32)

    def weigh(t, carry):
        at = pl.ds(pl.multiple_of(t * part, part), part)
        factor, square = factor_scr[at, :], square_scr[at, :]
        total = jnp.zeros((part, LANES), jnp.float32)
        for c in range(n_sim * groups):
            weight = jnp.exp2(factor * (square + value_scr[c, at, :]))
            weight_out[c // groups, at, c % groups * LANES : (c % groups + 1) * LANES] = weight.astype(jnp.bfloat16)
            total += weight
        total_out[at, :] = total
        return carry

    lax.fori_loop(0, n_obs // part, weigh, 0)
    total_out[...] = jnp.broadcast_to(jnp.sum(total_out[...], axis=1, keepdims=True), total_out.shape)


def product_kernel(columns, first, last, weight, *refs):
    blocks, rest, out = refs[: len(columns)], refs[len(columns) : -1], refs[-1]
    so_far = None if first else rest[-1]
    total_ref = rest[0] if last else None
    cells = out.shape[1]
    step = min(cells, 256)
    for j in range(cells // step):
        at = slice(j * step, (j + 1) * step)
        total = None if so_far is None else so_far[:, at]
        for column, block in zip(columns, blocks):
            term = jnp.dot(
                weight[column], block[:, at], preferred_element_type=jnp.float32
            )
            total = term if total is None else total + term
        if total_ref is not None:
            total = total / total_ref[:, :1]
        out[:, at] = total.astype(out.dtype)


def call(kernel, vmem, **kw):
    return pl.pallas_call(kernel, compiler_params=pltpu.CompilerParams(vmem_limit_bytes=vmem << 20), **kw)


def per_device(n_row, n_col, obs_summaries, sim_summaries, neighbours, field):
    f32, bf16 = jnp.float32, jnp.bfloat16
    rows, dims = obs_summaries.shape
    depth, cells = field.shape

    index = neighbours.T
    codes = jnp.concatenate([index // LANES, index % LANES], axis=0).astype(bf16)
    work = Work(ORDER if (n_row, n_col) == (16, 2) else {})
    names, at_blocks, at_obs, at_codes, table = share_sims(work, sim_summaries, obs_summaries, codes, n_row, n_col)
    n_sim, n_obs = n_row, n_col * rows
    kinds = kinds_of_place(n_row, n_col, table)
    weigh = call(
        functools.partial(
            weight_kernel, at_blocks, at_obs, at_codes, kinds, depth, rows, neighbours.shape[1], len(names)
        ),
        40,
        in_specs=[VMEM] * len(names),
        out_specs=[VMEM] * 2,
        out_shape=[
            jax.ShapeDtypeStruct((n_sim, n_obs, depth), bf16),
            jax.ShapeDtypeStruct((n_obs, LANES), f32),
        ],
        scratch_shapes=[
            pltpu.VMEM((n_obs, dims), bf16),
            pltpu.VMEM((n_obs, LANES), jnp.int32),
            pltpu.VMEM((n_obs, LANES), jnp.int32),
            pltpu.VMEM((n_sim * depth // LANES, n_obs, LANES), f32),
            pltpu.VMEM((n_obs, LANES), f32),
            pltpu.VMEM((n_obs, LANES), f32),
            pltpu.SMEM((n_sim,), jnp.int32),
        ],
        cost_estimate=SMALL,
        name="weights",
    )
    work.add("K", lambda: [work.get(name) for name in names], lambda arrays: weigh(*arrays))

    n_half = n_sim // 2
    work.add("F0", lambda: field, lambda value: value)
    for k, (sent, pairs) in enumerate(gather_steps(n_row)):
        work.add(
            f"F{k + 1}",
            lambda sent=sent: work.get(f"F{sent}"),
            lambda value, pairs=pairs: lax.ppermute(value, "row", pairs),
        )
    for k in range(n_half):
        work.add(f"D{k}", lambda k=k: work.get(f"F{k}"), lambda value: swap(value, "row", n_row, CORE_BIT))

    def product(columns, done, parts):
        (weight, total), before, held = parts
        extra = ([total] if done else []) + ([] if before is None else [before])
        return call(
            functools.partial(product_kernel, columns, before is None, done),
            28,
            in_specs=[VMEM] * (1 + len(held) + len(extra)),
            out_specs=VMEM,
            out_shape=jax.ShapeDtypeStruct((n_obs, cells), bf16 if done else f32),
            cost_estimate=SMALL,
            name="product",
        )(weight, *held, *extra)

    groups = GROUPS if n_half == sum(GROUPS) + 1 else (n_half // 2, n_half - n_half // 2 - 1)
    ends = [sum(groups[:g]) for g in range(len(groups) + 1)]
    groups = [[f"{what}{k}" for what in "FD" for k in range(*at)] for at in zip(ends[:-1], ends[1:])]
    groups += [[f"F{n_half - 1}"], [f"D{n_half - 1}"]]
    for g, group in enumerate(groups):
        columns = [int(name[1:]) + (n_half if name[0] == "D" else 0) for name in group]
        work.add(
            f"P{g + 1}",
            lambda g=g, group=group: (
                work.get("K"),
                work.get(f"P{g}") if g else None,
                [work.get(name) for name in group],
            ),
            lambda parts, columns=columns, done=g == len(groups) - 1: product(columns, done, parts),
        )
    return work.get(f"P{len(groups)}")


def solution(mesh):
    return jax.shard_map(
        functools.partial(per_device, mesh.shape["row"], mesh.shape["col"]),
        mesh=mesh,
        in_specs=(
            P(("row", "col"), None),
            P("row", None),
            P(("row", "col"), None),
            P("row", "col"),
        ),
        out_specs=P("row", "col"),
        check_vma=False,
    )
```
